32 devices in a mesh: grp: 4 (over y, core), sp: 8 (over z, x).
Axes of the slice: x: 2, y: 2, z: 4, core: 2. Of those that a mesh axis runs over, the one named last changes fastest.
Arguments:
- residual: bfloat16 [2048, 4096], P(('grp', 'sp')), may hold values from -6 to 6
- queries: bfloat16 [2048, 4096], P(('grp', 'sp')), may hold values from -60 to 60
- key_value_pairs: bfloat16 [2048, 1024], P(('grp', 'sp')), may hold values from -5 to 5
- out_weight: bfloat16 [4096, 4096], P('sp'), may hold values from -0.09375 to 0.09375
- norm_gain: float32 [4096], replicated, may hold values from 0.5 to 1.5
- amax_history: float32 [4], replicated, may hold values from 2 to 3.5
- doc_ids: int32 [4, 512], P('grp', 'sp'), may hold values from 0 to 5, never falling along the last dimension, each value on 1 to 192 neighbouring positions
- expert_ids: int32 [2048, 8], P(('grp', 'sp')), may hold values from 0 to 15, all different within a row; in each aligned block of 64 rows (0 to 63, 64 to 127, ...) at most 32 rows name the same one
- gate_up_weight: bfloat16 [32, 4096, 768], P(('grp', 'sp')), may hold values from -0.09375 to 0.09375
Outputs:
- after_attention: bfloat16 [2048, 4096], P(('grp', 'sp'))
- expert_hidden: bfloat16 [32, 1024, 384], P(('grp', 'sp'))
- group_amax: float32 [4], P('grp')
The draws below stay inside these ranges and needn't reach their ends.
Inputs may be any that keep to these rules, and one draw needn't show every extreme that they name: `doc_ids`: within a slice the document number never falls along the tokens. `expert_ids`: the 8 experts of a token are distinct. Among the 64 tokens of one device no expert is named more than 32 times, and on some device some expert is named exactly 32 times.
All inputs are finite; a program needn't handle non-finite values.
Results may differ from the reference program's by a relative error of at most 0.017.
Values may be sent and summed in bfloat16 or wider, within the bound.
A program may use at most 128 MiB of HBM per device.

```python
import math
import jax
import jax.numpy as jnp
import numpy as np
from jax import lax

D = 4096
QUERY_HEAD_SLICE = 32
KEY_VALUE_HEADS = 4
HEAD_SIZE = 128
TOP = 8
HALVES = 2
FFH = 384
DOCS = 6
TOK_DEV = 64
SLICE_TOKENS = 512
TOKEN_TOTAL = 2048
EXPERTS = 16
MOST = 32
SLOTS = 1024
N_GRP = 4
N_SP = 8
DEVICES = 32


def key_field(key):
    return jnp.clip(jax.random.normal(key, (TOKEN_TOTAL, KEY_VALUE_HEADS, HEAD_SIZE), jnp.float32), -3.0, 3.0)


def draw_queries(key, part):
    key = jax.random.fold_in(key, 7)
    values = jnp.clip(jax.random.normal(key, (TOKEN_TOTAL, QUERY_HEAD_SLICE, HEAD_SIZE), jnp.float32), -4.0, 4.0)
    return values.reshape(TOKEN_TOTAL, QUERY_HEAD_SLICE * HEAD_SIZE).astype(jnp.bfloat16)


def draw_key_value_pairs(key, part):
    keys_part = key_field(key)
    key = jax.random.fold_in(key, 11)
    value_portion = jnp.clip(jax.random.normal(key, (TOKEN_TOTAL, KEY_VALUE_HEADS, HEAD_SIZE), jnp.float32), -3.0, 3.0)
    joined_parts = jnp.stack([keys_part, value_portion], axis=2)
    return joined_parts.reshape(TOKEN_TOTAL, 2 * KEY_VALUE_HEADS * HEAD_SIZE).astype(jnp.bfloat16)


def levels(key, shape, cuts, low, top_value):
    def one(position, blocks):
        steps = jax.random.uniform(jax.random.fold_in(jax.random.fold_in(key, 6), position), (blocks,), jnp.float32, low / len(cuts), top_value / len(cuts))
        return jnp.repeat(jnp.exp(steps), shape[position] // blocks).reshape((-1,) + (1,) * (len(shape) - position - 1))

    factor_of = one(*cuts[0])
    for cut in cuts[1:]:
        factor_of = factor_of * one(*cut)
    return factor_of


def split_up(amount, total, limit, slope):
    weights = [(1 << 20) // math.isqrt(standing ** slope) + 1 for standing in range(2, amount + 1)]
    surplus, given = total - limit - (amount - 1), [1] * (amount - 1)
    while surplus > 0:
        movable = [i for i in range(amount - 1) if given[i] < limit]
        pool, left = sum([weights[i] for i in movable]), surplus
        for i in movable:
            more = min(limit - given[i], max(1, left * weights[i] // pool), surplus)
            given[i] = given[i] + more
            surplus = surplus - more
    return np.array([limit] + given)


def ragged(rng, number_of, total, bound, skew):
    if number_of == 2:
        one = jax.random.randint(rng, (), max(1, total - bound), min(bound, total - 1) + 1)
        return jnp.stack([one, total - one])
    lengths = jnp.asarray(split_up(number_of, total, bound, skew), jnp.int32)
    pairs = (number_of - 1) // 2
    donor, receiver = lengths[1:1 + 2 * pairs:2], lengths[2:2 + 2 * pairs:2]
    margin = jnp.minimum(donor - 1, bound - receiver)
    passed = jax.random.randint(jax.random.fold_in(rng, 1), (pairs,), 0, 1 << 20) % (margin + 1)
    lengths = lengths.at[1:1 + 2 * pairs:2].set(donor - passed).at[2:2 + 2 * pairs:2].set(receiver + passed)
    return lengths[jax.random.permutation(jax.random.fold_in(rng, 2), number_of)]


def shared_out(own_key, own, number, rows, amount, top, reach, skew):
    sequence = jax.random.permutation(own_key, amount)
    crowded, ordinary = shares(amount, rows * top, reach, skew, True), shares(amount, rows * top, reach, skew, False)
    places = jnp.arange(amount)

    def named(lengths, rotation):
        used = int((lengths > 0).sum())
        fixed = max(1, used // 4)
        passed = fixed + (places - fixed + rotation * (used - fixed)) % max(1, amount - fixed)
        return jnp.zeros((amount,), jnp.int32).at[sequence[jnp.where(places < fixed, places, passed)]].set(jnp.asarray(lengths, jnp.int32))

    lengths = jnp.where(number % 4 == 0, named(crowded, number // 4), named(ordinary, number - number // 4 - 1))
    mixed = jax.random.permutation(jax.random.fold_in(own, 3), amount)
    giver, sink = mixed[0:amount // 2 * 2:2], mixed[1:amount // 2 * 2:2]
    margin = jnp.minimum(lengths[giver] - 1, reach - lengths[sink]) // 2
    margin = jnp.where((giver == sequence[0]) | (sink == sequence[0]) | (lengths[sink] == 0), 0, jnp.maximum(margin, 0))
    passed = jax.random.randint(jax.random.fold_in(own, 4), (amount // 2,), 0, 1 << 20) % (margin + 1)
    lengths = lengths.at[giver].add(-passed).at[sink].add(passed)
    labels = jnp.searchsorted(jnp.cumsum(lengths), jnp.arange(rows * top), side="right").astype(jnp.int32)
    table = labels.reshape(top, rows).T
    table = table[jax.random.permutation(jax.random.fold_in(own, 1), rows)]
    rotation = jax.random.randint(jax.random.fold_in(own, 2), (rows, 1), 0, top)
    return jnp.take_along_axis(table, (jnp.arange(top)[None, :] + rotation) % top, axis=1)


def shares(amount, total, most, lean, full):
    loads = [(1 << 20) // math.isqrt(rank ** lean) + 1 for rank in range(1, amount + 1)]
    largest = most if full else min(most, max(-(-total // amount), total * loads[0] // sum(loads)))
    least = 1 if total - largest >= amount - 1 else 0
    given, surplus = [largest] + [least] * (amount - 1), total - largest - least * (amount - 1)
    while surplus > 0:
        candidates = [i for i in range(1, amount) if given[i] < largest] or [i for i in range(1, amount) if given[i] < most]
        mass, left = sum([loads[i] for i in candidates]), surplus
        for i in candidates:
            addition = min(most - given[i], max(1, left * loads[i] // mass), surplus)
            given[i] = given[i] + addition
            surplus = surplus - addition
    return np.array(given)


def scatter_about(stream_key, shape, scale, limit, shards=(), kind=jnp.bfloat16):
    array = jax.random.normal(stream_key, shape, jnp.float32) * scale
    if len(shards) > 0:
        array = levels(stream_key, shape, shards, -0.22, 0.18) * array
    return jnp.clip(array, min=-limit, max=limit).astype(kind)


def setup_inputs(seed: int = 0) -> dict:
    splits = jax.random.split(jax.random.key(seed), 10)
    residual = scatter_about(splits[0], (TOKEN_TOTAL, D), 1.0, 6.0, ((0, 32),))
    queries = draw_queries(jax.random.fold_in(splits[9], 71), 0)
    key_value_pairs = draw_key_value_pairs(jax.random.fold_in(splits[9], 71), 0)
    out_weight = scatter_about(splits[3], (QUERY_HEAD_SLICE * HEAD_SIZE, D), (QUERY_HEAD_SLICE * HEAD_SIZE) ** -0.5, 0.09375, ((0, 8),))
    norm_gain = jnp.clip(1.0 + 0.1 * jax.random.normal(splits[4], (D,), jnp.float32), 0.5, 1.5)
    amax_history = jnp.clip(jax.random.uniform(splits[5], (N_GRP,), jnp.float32, 2.0, 3.5), 2.0, 3.5)
    doc_ids = jax.vmap(lambda own: jnp.searchsorted(jnp.cumsum(ragged(own, DOCS, SLICE_TOKENS, SLICE_TOKENS * 3 // 8, 1)), jnp.arange(SLICE_TOKENS), side="right"))(jax.random.split(splits[6], N_GRP)).reshape((N_GRP, SLICE_TOKENS)).astype(jnp.int32)
    expert_ids_keys = jax.random.split(jax.random.fold_in(splits[7], 1), TOKEN_TOTAL // TOK_DEV)
    expert_ids_turns = jax.random.permutation(jax.random.fold_in(splits[7], 3), TOKEN_TOTAL // TOK_DEV)
    expert_ids = jax.vmap(lambda own, number: shared_out(jax.random.fold_in(splits[7], 2), own, number, TOK_DEV, EXPERTS, TOP, MOST, 0))(expert_ids_keys, expert_ids_turns).reshape((TOKEN_TOTAL, TOP))
    gate_up_weight = scatter_about(splits[8], (EXPERTS * HALVES, D, 2 * FFH), D ** -0.5, 0.09375, ((0, 32),))
    return {"residual": residual, "queries": queries, "key_value_pairs": key_value_pairs, "out_weight": out_weight, "norm_gain": norm_gain, "amax_history": amax_history, "doc_ids": doc_ids, "expert_ids": expert_ids, "gate_up_weight": gate_up_weight}


def attend_group(query_group, pair_group, doc_group):
    positions = jnp.arange(SLICE_TOKENS, dtype=jnp.int32)
    allowed = (positions[None, :] <= positions[:, None]) & (doc_group[None, :] == doc_group[:, None])
    group_width = QUERY_HEAD_SLICE // KEY_VALUE_HEADS

    def one_head(head):
        query_rows = lax.dynamic_index_in_dim(query_group, head, 1, False)
        pair_rows = lax.dynamic_index_in_dim(pair_group, head // group_width, 1, False)
        scores = jnp.dot(query_rows, pair_rows[:, 0].T, preferred_element_type=jnp.float32) * HEAD_SIZE ** (-0.5)
        scores = jnp.where(allowed, scores, -jnp.inf)
        highest = lax.optimization_barrier(jnp.max(scores, axis=1, keepdims=True))
        weights = jnp.exp(scores - highest)
        probs = (weights / lax.optimization_barrier(jnp.sum(weights, axis=1, keepdims=True))).astype(jnp.bfloat16)
        return jnp.dot(probs, pair_rows[:, 1], preferred_element_type=jnp.float32).astype(jnp.bfloat16)
    context = lax.map(one_head, jnp.arange(QUERY_HEAD_SLICE, dtype=jnp.int32))
    return jnp.transpose(context, (1, 0, 2)).reshape(SLICE_TOKENS, QUERY_HEAD_SLICE * HEAD_SIZE)

def reference(residual, queries, key_value_pairs, out_weight, norm_gain, amax_history, doc_ids, expert_ids, gate_up_weight):
    query_all = queries.reshape(N_GRP, SLICE_TOKENS, QUERY_HEAD_SLICE, HEAD_SIZE)
    pair_gathered = key_value_pairs.reshape(N_GRP, SLICE_TOKENS, KEY_VALUE_HEADS, 2, HEAD_SIZE)
    context = lax.map(lambda parts: attend_group(parts[0], parts[1], parts[2]), (query_all, pair_gathered, doc_ids))
    block_width = QUERY_HEAD_SLICE * HEAD_SIZE // N_SP
    context = context.reshape(TOKEN_TOTAL, N_SP, block_width)
    weight_blocks = out_weight.reshape(N_SP, block_width, D)

    def add_block(index, total):
        columns = lax.dynamic_index_in_dim(context, index, 1, False)
        rows = lax.dynamic_index_in_dim(weight_blocks, index, 0, False)
        term = jnp.dot(columns, rows, preferred_element_type=jnp.float32).astype(jnp.bfloat16)
        term = lax.optimization_barrier(term)
        return total + term.astype(jnp.float32)
    projected = lax.fori_loop(0, N_SP, add_block, jnp.zeros((TOKEN_TOTAL, D), jnp.float32))
    after_attention = (residual.astype(jnp.float32) + projected).astype(jnp.bfloat16)
    widened = after_attention.astype(jnp.float32)
    normed = widened * lax.rsqrt(lax.optimization_barrier(jnp.mean(widened * widened, axis=1, keepdims=True)) + 1e-06) * norm_gain
    group_amax = lax.optimization_barrier(jnp.max(jnp.abs(normed).reshape(N_GRP, SLICE_TOKENS * D), axis=1))
    token_group = jnp.arange(TOKEN_TOTAL, dtype=jnp.int32) // SLICE_TOKENS
    scale = (448.0 / amax_history)[token_group][:, None]
    quantized = jnp.clip(normed * scale, -448.0, 448.0).astype(jnp.bfloat16)
    routing = expert_ids.reshape(DEVICES, TOK_DEV * TOP)
    one_hot = (routing[:, :, None] == jnp.arange(EXPERTS, dtype=jnp.int32)[None, None, :]).astype(jnp.int32)
    earlier = jnp.cumsum(one_hot, axis=1) - one_hot
    rank = lax.optimization_barrier(jnp.sum(earlier * one_hot, axis=2))
    device_index = jnp.arange(DEVICES, dtype=jnp.int32)[:, None]
    flat_slot = routing * SLOTS + device_index * MOST + rank
    token_index = device_index * TOK_DEV + jnp.arange(TOK_DEV * TOP, dtype=jnp.int32)[None, :] // TOP
    slot_table = jnp.full((EXPERTS * SLOTS,), -1, jnp.int32)
    slot_table = slot_table.at[flat_slot.reshape(-1)].set(token_index.reshape(-1)).reshape(EXPERTS, SLOTS)
    slot_group = jnp.arange(SLOTS, dtype=jnp.int32) // MOST // N_SP
    unscale = (amax_history / 448.0)[slot_group][:, None]
    weights_all = gate_up_weight.reshape(EXPERTS, HALVES, D, 2 * FFH)

    def one_expert(parts):
        sources, expert_weights = parts
        valid = sources >= 0
        rows = jnp.where(valid[:, None], quantized[jnp.maximum(sources, 0)], jnp.zeros((), quantized.dtype))

        def one_half(half_weight):
            gate_up = jnp.dot(rows, half_weight, preferred_element_type=jnp.float32)
            gate = gate_up[:, :FFH] * unscale
            upward = gate_up[:, FFH:] * unscale
            return (jax.nn.silu(gate) * upward).astype(jnp.bfloat16)
        return lax.map(one_half, expert_weights)
    expert_hidden = lax.map(one_expert, (slot_table, weights_all)).reshape(EXPERTS * HALVES, SLOTS, FFH)
    return (after_attention, expert_hidden, group_amax)
```

```python
import jax
import jax.numpy as jnp
from jax import lax
from jax.experimental import pallas as pl
from jax.experimental.pallas import tpu as pltpu
from jax.sharding import PartitionSpec as P

QUERY_HEAD_SLICE = 32
KEY_VALUE_HEADS = 4
HEAD_SIZE = 128
TOP = 8
HALVES = 2


def activate(rows, unscale, weight):
    width = weight.shape[1] // 2
    gate_up = jnp.dot(rows, weight, preferred_element_type=jnp.float32)
    gate = gate_up[:, :width] * unscale
    upward = gate_up[:, width:] * unscale
    return (jax.nn.silu(gate) * upward).astype(jnp.bfloat16)


def copy_to(source, target, send, receive, device):
    return pltpu.make_async_remote_copy(
        src_ref=source,
        dst_ref=target,
        send_sem=send,
        recv_sem=receive,
        device_id=device,
        device_id_type=pl.DeviceIdType.MESH,
    )


def back_kernel(
    context_ref,
    residual_ref,
    gain_ref,
    history_ref,
    pick_ref,
    out_weight_ref,
    expert_weight_ref,
    after_ref,
    hidden_ref,
    amax_ref,
    out_weight,
    expert_weight,
    pair_send,
    pair_receive,
    line_send,
    line_receive,
    rows,
    amaxes,
    local_sem,
    pair_sems,
    line_send_sems,
    line_receive_sems,
    row_send_sems,
    row_receive_sems,
    amax_send_sems,
    amax_receive_sems,
):
    grp, sp = lax.axis_index("grp"), lax.axis_index("sp")
    y, core = grp // 2, grp % 2
    z, x = sp // 2, sp % 2
    tokens, model = residual_ref.shape
    chunks, _, chunk = pair_send.shape
    width = hidden_ref.shape[1]
    most = pick_ref.shape[1]

    def device(x, y, core, z):
        return (2 * y + core, 2 * z + x)

    def slot(x, y, core, z):
        return ((y * 2 + x) * 2 + core) * 4 + z

    def block(place):
        return rows.at[pl.ds(pl.multiple_of(place * tokens, tokens), tokens)]

    def z_peer(step):
        return lax.rem(z + step, 4)

    sibling = device(x, y, 1 - core, z)
    x_peer = device(1 - x, y, core, z)
    y_peer = device(x, 1 - y, core, z)

    def weight_chunk(k):
        columns = pl.ds(pl.multiple_of(k * chunk, chunk), chunk)
        return pltpu.make_async_copy(
            out_weight_ref.at[:, columns], out_weight.at[k], local_sem.at[k]
        )

    expert_copy = pltpu.make_async_copy(expert_weight_ref, expert_weight, local_sem.at[chunks])
    for k in range(chunks):
        weight_chunk(k).start()
    expert_copy.start()

    barrier = pltpu.get_barrier_semaphore()
    partners = [sibling, x_peer, y_peer]
    for step in (1, 2, 3):
        partners.append(device(x, y, core, z_peer(step)))
        partners.append(device(1 - x, y, core, z_peer(step)))
    for partner in partners:
        pl.semaphore_signal(
            barrier, inc=1, device_id=partner, device_id_type=pl.DeviceIdType.MESH
        )
    pl.semaphore_wait(barrier, len(partners))

    def pair_copy(k):
        return copy_to(
            pair_send.at[k], pair_receive.at[k], pair_sems.at[0, k], pair_sems.at[1, k], x_peer
        )

    def send_pair(k, carry):
        weight_chunk(k).wait()
        term = jnp.dot(context_ref[1 - x], out_weight[k], preferred_element_type=jnp.float32)
        pair_send[k] = term.astype(jnp.bfloat16)
        pair_copy(k).start()
        return carry

    lax.fori_loop(0, chunks, send_pair, 0)

    def line_copy(k, step):
        target = z_peer(step)
        source = line_send.at[k, pl.ds(pl.multiple_of(target * tokens, tokens), tokens)]
        return copy_to(
            source,
            line_receive.at[k, step - 1],
            line_send_sems.at[k, step - 1],
            line_receive_sems.at[k, step - 1],
            device(x, y, core, target),
        )

    def send_line(k, carry):
        term = jnp.dot(context_ref[x], out_weight[k], preferred_element_type=jnp.float32)
        pair_copy(k).wait_recv()
        line_send[k] = (term + pair_receive[k].astype(jnp.float32)).astype(jnp.bfloat16)
        for step in (2, 1, 3):
            line_copy(k, step).start()
        return carry

    lax.fori_loop(0, chunks, send_line, 0)

    def finish(k, squares):
        columns = pl.ds(pl.multiple_of(k * chunk, chunk), chunk)
        total = line_send[k, pl.ds(pl.multiple_of(z * tokens, tokens), tokens)].astype(jnp.float32)
        for step in (1, 3, 2):
            line_copy(k, step).wait_recv()
            total = total + line_receive[k, step - 1].astype(jnp.float32)
        after = (residual_ref[:, columns].astype(jnp.float32) + total).astype(jnp.bfloat16)
        after_ref[:, columns] = after
        widened = after.astype(jnp.float32)
        return squares + jnp.sum(widened * widened, axis=1, keepdims=True)

    squares = lax.fori_loop(0, chunks, finish, jnp.zeros((tokens, 1), jnp.float32))
    inverse = lax.rsqrt(squares / model + 1e-06)
    scale = 448.0 / history_ref[grp]
    own_rows = pl.ds(pl.multiple_of(slot(x, y, core, z) * tokens, tokens), tokens)

    def normalize(k, highest):
        columns = pl.ds(pl.multiple_of(k * chunk, chunk), chunk)
        normed = after_ref[:, columns].astype(jnp.float32) * inverse * gain_ref[:, columns]
        rows[own_rows, columns] = jnp.clip(normed * scale, -448.0, 448.0).astype(jnp.bfloat16)
        return jnp.maximum(highest, jnp.max(jnp.abs(normed), axis=1, keepdims=True))

    highest = lax.fori_loop(0, chunks, normalize, jnp.zeros((tokens, 1), jnp.float32))

    started = []

    def pass_on(place, target, half=None, landing=0):
        source = block(place)
        if half is not None:
            source = source.at[pl.ds(half * (tokens // 2), tokens // 2)]
        started.append(
            copy_to(
                source,
                source,
                row_send_sems.at[len(started)],
                row_receive_sems.at[place, landing],
                target,
            )
        )
        started[-1].start()

    def arrived(place, half=None, landing=0):
        source = block(place)
        if half is not None:
            source = source.at[pl.ds(half * (tokens // 2), tokens // 2)]
        copy_to(
            source, source, row_send_sems.at[0], row_receive_sems.at[place, landing], sibling
        ).wait_recv()

    own = slot(x, y, core, z)
    pass_on(own, x_peer)
    pass_on(own, y_peer)
    for step in (1, 3, 2):
        pass_on(own, device(x, y, core, z_peer(step)))
    pass_on(own, sibling)

    amaxes[sp] = jnp.broadcast_to(jnp.max(highest, axis=0, keepdims=True), amaxes.shape[1:])

    def amax_copy(step):
        target = lax.rem(sp + step, 8)
        return copy_to(
            amaxes.at[sp],
            amaxes.at[sp],
            amax_send_sems.at[step - 1],
            amax_receive_sems.at[step - 1],
            (grp, target),
        )

    for step in range(1, 8):
        amax_copy(step).start()

    for step in (1, 3, 2):
        place = slot(x, y, core, z_peer(step))
        arrived(place)
        pass_on(place, x_peer)
        pass_on(place, y_peer)
        pass_on(place, sibling)

    expert_copy.wait()

    def compute(index, carry):
        other_core = lax.rem(core + index, 2)
        other_x = lax.rem(x + index // 2, 2)
        other_y = lax.rem(y + index // 4, 2)
        first = pl.multiple_of(slot(other_x, other_y, other_core, 0) * tokens, 4 * tokens)
        gate_up = jnp.dot(
            rows[pl.ds(first, 4 * tokens)], expert_weight[...], preferred_element_type=jnp.float32
        )
        source = 2 * other_y + other_core
        unscale = history_ref[source] / 448.0
        gate = gate_up[:, :width] * unscale
        upward = gate_up[:, width:] * unscale
        hidden = (gate / (1.0 + jnp.exp(-gate)) * upward).astype(jnp.bfloat16)
        for line in range(4):
            origin = source * 8 + 2 * line + other_x
            picked = jnp.dot(
                pick_ref[origin],
                hidden[line * tokens : (line + 1) * tokens],
                preferred_element_type=jnp.float32,
            )
            hidden_ref[pl.ds(pl.multiple_of(origin * most, most), most)] = picked.astype(
                jnp.bfloat16
            )
        return carry

    def sibling_group(x, y):
        for line in range(4):
            arrived(slot(x, y, 1 - core, line))

    lax.fori_loop(0, 1, compute, 0)
    sibling_group(x, y)
    lax.fori_loop(1, 2, compute, 0)

    for step in (0, 1, 3, 2):
        place = slot(1 - x, y, core, z_peer(step))
        arrived(place)
        pass_on(place, y_peer, 0, 0)
        pass_on(place, sibling)
        place = slot(x, 1 - y, core, z_peer(step))
        arrived(place)
        pass_on(place, x_peer, 1, 1)
        pass_on(place, sibling)
    sibling_group(1 - x, y)
    sibling_group(x, 1 - y)
    lax.fori_loop(2, 6, compute, 0)

    for step in (0, 1, 3, 2):
        place = slot(1 - x, 1 - y, core, z_peer(step))
        arrived(place, 0, 0)
        arrived(place, 1, 1)
        pass_on(place, sibling)
    lax.fori_loop(6, 7, compute, 0)
    sibling_group(1 - x, 1 - y)
    lax.fori_loop(7, 8, compute, 0)

    for step in range(1, 8):
        amax_copy(step).wait_recv()
    amax_ref[...] = jnp.max(amaxes[...], axis=0)

    for step in range(1, 8):
        amax_copy(step).wait_send()
    for copy in started:
        copy.wait_send()

    def drain(k, carry):
        pair_copy(k).wait_send()
        for step in (1, 2, 3):
            line_copy(k, step).wait_send()
        return carry

    lax.fori_loop(0, chunks, drain, 0)


def back(context, residual, norm_gain, amax_history, picks, out_weight, expert_weight):
    tokens, model = residual.shape
    block_width = out_weight.shape[0]
    width = expert_weight.shape[1] // 2
    devices, most, _ = picks.shape
    chunks = 8
    chunk = model // chunks
    vmem = pl.BlockSpec(memory_space=pltpu.VMEM)
    smem = pl.BlockSpec(memory_space=pltpu.SMEM)
    hbm = pl.BlockSpec(memory_space=pl.ANY)
    dma = pltpu.SemaphoreType.DMA
    halves = jnp.transpose(context.reshape(4, 2, tokens, block_width), (1, 0, 2, 3))
    return pl.pallas_call(
        back_kernel,
        out_shape=(
            jax.ShapeDtypeStruct((tokens, model), jnp.bfloat16),
            jax.ShapeDtypeStruct((devices * most, width), jnp.bfloat16),
            jax.ShapeDtypeStruct((8, 128), jnp.float32),
        ),
        in_specs=[vmem, vmem, vmem, smem, vmem, hbm, hbm],
        out_specs=(vmem, vmem, vmem),
        scratch_shapes=[
            pltpu.VMEM((chunks, block_width, chunk), jnp.bfloat16),
            pltpu.VMEM(expert_weight.shape, jnp.bfloat16),
            pltpu.VMEM((chunks, 4 * tokens, chunk), jnp.bfloat16),
            pltpu.VMEM((chunks, 4 * tokens, chunk), jnp.bfloat16),
            pltpu.VMEM((chunks, 4 * tokens, chunk), jnp.bfloat16),
            pltpu.VMEM((chunks, 3, tokens, chunk), jnp.bfloat16),
            pltpu.VMEM((devices * tokens, model), jnp.bfloat16),
            pltpu.VMEM((8, 8, 128), jnp.float32),
            dma((chunks + 1,)),
            dma((2, chunks)),
            dma((chunks, 3)),
            dma((chunks, 3)),
            dma((35,)),
            dma((devices, 2)),
            dma((7,)),
            dma((7,)),
        ],
        compiler_params=pltpu.CompilerParams(
            collective_id=0, has_side_effects=True, vmem_limit_bytes=56 * 1024 * 1024
        ),
        cost_estimate=pl.CostEstimate(
            flops=2 * devices * tokens * model * 2 * width,
            bytes_accessed=12 * 1024 * 1024,
            transcendentals=devices * tokens * width,
        ),
        name="project_norm_dispatch",
    )(
        halves.reshape(2, 4 * tokens, block_width),
        residual,
        norm_gain.reshape(1, model),
        amax_history,
        picks,
        out_weight,
        expert_weight,
    )


def pick_rows(expert_ids, most_rows):
    local_row_count = expert_ids.shape[0]
    everyone = lax.all_gather(expert_ids, ("grp", "sp"), axis=0)
    expert = (
        lax.axis_index("grp") * (lax.axis_size("sp") // HALVES) + lax.axis_index("sp") // HALVES
    )
    named = jnp.any(everyone == expert, axis=2)
    order = jnp.arange(local_row_count, dtype=jnp.int32)
    earlier = (order[:, None] < order[None, :]).astype(jnp.bfloat16)
    rank = jnp.dot(named.astype(jnp.bfloat16), earlier, preferred_element_type=jnp.float32)
    slots = jnp.arange(most_rows, dtype=jnp.int32)
    chosen = named[:, None, :] & (rank.astype(jnp.int32)[:, None, :] == slots[None, :, None])
    return chosen.astype(jnp.bfloat16)


def per_device(
    residual,
    queries,
    key_value_pairs,
    out_weight,
    norm_gain,
    amax_history,
    doc_ids,
    expert_ids,
    gate_up_weight,
):
    sequence_parallel_count = lax.axis_size("sp")
    grp_count = lax.axis_size("grp")
    local_row_count = residual.shape[0]
    heads_here = QUERY_HEAD_SLICE // sequence_parallel_count
    query_local = queries.reshape(local_row_count, sequence_parallel_count, heads_here * HEAD_SIZE)
    pair_replicas = jnp.repeat(
        key_value_pairs.reshape(local_row_count, KEY_VALUE_HEADS, 2 * HEAD_SIZE),
        sequence_parallel_count // KEY_VALUE_HEADS,
        axis=1,
    )
    doc_copies = jnp.broadcast_to(
        doc_ids.reshape(local_row_count, 1, 1), (local_row_count, sequence_parallel_count, 1)
    )
    query_heads, pair_head, doc_column = (
        lax.all_to_all(query_local, "sp", split_axis=1, concat_axis=0, tiled=True),
        lax.all_to_all(pair_replicas, "sp", split_axis=1, concat_axis=0, tiled=True),
        lax.all_to_all(doc_copies, "sp", split_axis=1, concat_axis=0, tiled=True),
    )
    slice_length = query_heads.shape[0]
    pair_head = pair_head.reshape(slice_length, 2 * HEAD_SIZE)
    documents = doc_column.reshape(slice_length)
    query_heads = query_heads.reshape(slice_length, heads_here, HEAD_SIZE)
    key_rows = pair_head[:, :HEAD_SIZE]
    value_rows = pair_head[:, HEAD_SIZE:]
    block_rows = min(512, slice_length)
    positions = jnp.arange(slice_length, dtype=jnp.int32)

    def attend(block_index):
        offset = block_index * block_rows
        query_block = lax.dynamic_slice_in_dim(query_heads, offset, block_rows, 0)
        row_positions = offset + jnp.arange(block_rows, dtype=jnp.int32)
        row_documents = lax.dynamic_slice_in_dim(documents, offset, block_rows, 0)
        allowed = (positions[None, :] <= row_positions[:, None]) & (
            documents[None, :] == row_documents[:, None]
        )
        scores = jnp.einsum(
            "bhd,kd->hbk", query_block, key_rows, preferred_element_type=jnp.float32
        ) * HEAD_SIZE ** (-0.5)
        scores = jnp.where(allowed[None], scores, -jnp.inf)
        highest = jnp.max(scores, axis=2, keepdims=True)
        weights = jnp.exp(scores - highest)
        probs = (weights / jnp.sum(weights, axis=2, keepdims=True)).astype(jnp.bfloat16)
        return jnp.einsum(
            "hbk,kd->bhd", probs, value_rows, preferred_element_type=jnp.float32
        ).astype(jnp.bfloat16)

    context = lax.map(attend, jnp.arange(slice_length // block_rows, dtype=jnp.int32))
    block_width = heads_here * HEAD_SIZE
    context = context.reshape(slice_length, block_width)
    experts = grp_count * sequence_parallel_count // HALVES
    most_rows = max(2, local_row_count * TOP // experts)
    if (grp_count, sequence_parallel_count) == (4, 8):
        after_attention, expert_hidden, highest = back(
            context,
            residual,
            norm_gain,
            amax_history,
            pick_rows(expert_ids, most_rows),
            out_weight,
            gate_up_weight[0],
        )
        return after_attention, expert_hidden[None], highest[0, :1]
    projected = lax.psum_scatter(
        jnp.dot(context, out_weight, preferred_element_type=jnp.float32).astype(jnp.bfloat16),
        "sp",
        scatter_dimension=0,
        tiled=True,
    ).astype(jnp.float32)
    after_attention = (residual.astype(jnp.float32) + projected).astype(jnp.bfloat16)
    widened = after_attention.astype(jnp.float32)
    normed = (
        widened * lax.rsqrt(jnp.mean(widened * widened, axis=1, keepdims=True) + 1e-06) * norm_gain
    )
    group_amax = lax.pmax(jnp.max(jnp.abs(normed)).reshape(1), "sp")
    own_history = lax.dynamic_index_in_dim(amax_history, lax.axis_index("grp"), 0, False)
    quantized = jnp.clip(normed * (448.0 / own_history), -448.0, 448.0).astype(jnp.bfloat16)
    routing = expert_ids.reshape(local_row_count * TOP)
    one_hot = (routing[:, None] == jnp.arange(experts, dtype=jnp.int32)[None, :]).astype(jnp.int32)
    rank = jnp.sum((jnp.cumsum(one_hot, axis=0) - one_hot) * one_hot, axis=1)
    slot_index = routing * most_rows + rank
    picker = jnp.arange(experts * most_rows, dtype=jnp.int32)[:, None] == slot_index[None, :]
    picker = jnp.sum(
        picker.reshape(experts * most_rows, local_row_count, TOP).astype(jnp.int32), axis=2
    ).astype(jnp.bfloat16)
    outgoing = jnp.dot(picker, quantized, preferred_element_type=jnp.float32).astype(jnp.bfloat16)
    outgoing = outgoing.reshape(grp_count, experts // grp_count, most_rows, outgoing.shape[1])
    arrived = lax.all_to_all(outgoing, "grp", split_axis=0, concat_axis=0, tiled=True)
    width_model = arrived.shape[3]
    copies = jnp.repeat(arrived, HALVES, axis=1)
    slot_rows = lax.all_to_all(copies, "sp", split_axis=1, concat_axis=1, tiled=True)
    total_rows = grp_count * sequence_parallel_count * most_rows
    flat_rows = slot_rows.reshape(total_rows, width_model)
    unscale = jnp.repeat(amax_history / 448.0, sequence_parallel_count * most_rows)[:, None]
    weight = gate_up_weight[0]
    expert_hidden = activate(flat_rows, unscale, weight)
    return (
        after_attention,
        expert_hidden.reshape(1, total_rows, expert_hidden.shape[1]),
        group_amax,
    )


def solution(mesh):
    in_specs = (
        P(("grp", "sp"), None),
        P(("grp", "sp"), None),
        P(("grp", "sp"), None),
        P("sp", None),
        P(),
        P(),
        P("grp", "sp"),
        P(("grp", "sp"), None),
        P(("grp", "sp"), None, None),
    )
    out_specs = (P(("grp", "sp"), None), P(("grp", "sp"), None, None), P("grp"))
    return jax.shard_map(
        per_device, mesh=mesh, in_specs=in_specs, out_specs=out_specs, check_vma=False
    )
```

```python
import jax
import jax.numpy as jnp
from jax import lax
from jax.experimental import pallas as pl
from jax.experimental.pallas import tpu as pltpu
from jax.sharding import PartitionSpec as P

QUERY_HEAD_SLICE = 32
KEY_VALUE_HEADS = 4
HEAD_SIZE = 128
TOP = 8
HALVES = 2


def activate(rows, unscale, weight):
    width = weight.shape[1] // 2
    gate_up = jnp.dot(rows, weight, preferred_element_type=jnp.float32)
    gate = gate_up[:, :width] * unscale
    upward = gate_up[:, width:] * unscale
    return (jax.nn.silu(gate) * upward).astype(jnp.bfloat16)


def copy_to(source, target, send, receive, device):
    return pltpu.make_async_remote_copy(
        src_ref=source,
        dst_ref=target,
        send_sem=send,
        recv_sem=receive,
        device_id=device,
        device_id_type=pl.DeviceIdType.MESH,
    )


def layer_kernel(
    queries_ref,
    pairs_ref,
    documents_ref,
    residual_ref,
    gain_ref,
    history_ref,
    ranks_ref,
    out_weight_ref,
    expert_weight_ref,
    after_ref,
    hidden_ref,
    amax_ref,
    query_rows,
    pair_rows,
    pair_blocks,
    context,
    out_weight,
    expert_weight,
    pair_send,
    pair_receive,
    line_send,
    line_receive,
    rows,
    amaxes,
    local_sem,
    pair_sems,
    line_send_sems,
    line_receive_sems,
    row_send_sems,
    row_receive_sems,
    amax_send_sems,
    amax_receive_sems,
    head_send_sems,
    head_receive_sems,
):
    grp, sp = lax.axis_index("grp"), lax.axis_index("sp")
    y, core = grp // 2, grp % 2
    z, x = sp // 2, sp % 2
    tokens, model = residual_ref.shape
    chunks, _, chunk = pair_send.shape
    width = hidden_ref.shape[1]
    most = hidden_ref.shape[0] * tokens // rows.shape[0]
    heads_width = query_rows.shape[1]
    nearest = (z, z + 1 - 2 * (z % 2), 2 - z // 2, 3 * (1 - z // 2))

    def device(x, y, core, z):
        return (2 * y + core, 2 * z + x)

    def slot(x, y, core, z):
        return ((y * 2 + x) * 2 + core) * 4 + z

    def block(place):
        return rows.at[pl.ds(pl.multiple_of(place * tokens, tokens), tokens)]

    def z_peer(step):
        return lax.rem(z + step, 4)

    sibling = device(x, y, 1 - core, z)
    x_peer = device(1 - x, y, core, z)
    y_peer = device(x, 1 - y, core, z)

    def weight_chunk(k):
        columns = pl.ds(pl.multiple_of(k * chunk, chunk), chunk)
        return pltpu.make_async_copy(
            out_weight_ref.at[:, columns], out_weight.at[k], local_sem.at[k]
        )

    expert_copy = pltpu.make_async_copy(expert_weight_ref, expert_weight, local_sem.at[chunks])
    for k in range(chunks):
        weight_chunk(k).start()
    expert_copy.start()

    for head in range(KEY_VALUE_HEADS):
        pair_blocks[head, :, : 2 * HEAD_SIZE] = pairs_ref[
            :, head * 2 * HEAD_SIZE : (head + 1) * 2 * HEAD_SIZE
        ]
        pair_blocks[head, :, 2 * HEAD_SIZE :] = documents_ref[...]

    barrier = pltpu.get_barrier_semaphore()
    partners = [sibling, x_peer, y_peer]
    for step in (1, 2, 3):
        partners.append(device(x, y, core, z_peer(step)))
        partners.append(device(1 - x, y, core, z_peer(step)))
    for partner in partners:
        pl.semaphore_signal(
            barrier, inc=1, device_id=partner, device_id_type=pl.DeviceIdType.MESH
        )
    pl.semaphore_wait(barrier, len(partners))

    def token_rows(member):
        place = (member % 2) * 4 + member // 2
        return pl.ds(pl.multiple_of(place * tokens, tokens), tokens)

    def query_columns(member):
        return queries_ref.at[
            :, pl.ds(pl.multiple_of(member * heads_width, heads_width), heads_width)
        ]

    def head_copies(step, origin):
        target = lax.rem(sp + step, 8)
        return (
            copy_to(
                pair_blocks.at[target // 2],
                pair_rows.at[token_rows(origin)],
                head_send_sems.at[0, step - 1],
                head_receive_sems.at[0, step - 1],
                (grp, target),
            ),
            copy_to(
                query_columns(target),
                query_rows.at[token_rows(origin)],
                head_send_sems.at[1, step - 1],
                head_receive_sems.at[1, step - 1],
                (grp, target),
            ),
        )

    for step in range(1, 8):
        for copy in head_copies(step, sp):
            copy.start()
    own_queries = pltpu.make_async_copy(
        query_columns(sp), query_rows.at[token_rows(sp)], local_sem.at[chunks + 1]
    )
    own_queries.start()
    pair_rows[token_rows(sp)] = pair_blocks[sp // 2]
    own_queries.wait()
    for step in range(1, 8):
        for copy in head_copies(step, lax.rem(sp + 8 - step, 8)):
            copy.wait_recv()

    def attend(half):
        count = 4 * tokens
        here = pl.ds(pl.multiple_of(half * count, count), count)
        row = lax.broadcasted_iota(jnp.int32, (count, 1), 0)
        column = lax.broadcasted_iota(jnp.int32, (1, 2 * count), 1)
        row_position = (lax.div(row, tokens) * 2 + half) * tokens + lax.rem(row, tokens)
        column_half = lax.div(column, count)
        column_place = lax.rem(column, count)
        column_position = (lax.div(column_place, tokens) * 2 + column_half) * tokens + lax.rem(
            column_place, tokens
        )
        lanes = slice(2 * HEAD_SIZE, 3 * HEAD_SIZE)
        first_lane = lax.broadcasted_iota(jnp.int32, (16, HEAD_SIZE), 1) == 0
        column_documents = lax.dot_general(
            first_lane.astype(jnp.bfloat16),
            pair_rows[:, lanes],
            (((1,), (1,)), ((), ())),
            preferred_element_type=jnp.float32,
        )[:1]
        row_documents = pair_rows[here, lanes].astype(jnp.float32)[:, :1]
        allowed = (column_position <= row_position) & (row_documents == column_documents)

        def one_head(head, carry):
            columns = pl.ds(pl.multiple_of(head * HEAD_SIZE, HEAD_SIZE), HEAD_SIZE)
            scores = lax.dot_general(
                query_rows[here, columns],
                pair_rows[:, :HEAD_SIZE],
                (((1,), (1,)), ((), ())),
                preferred_element_type=jnp.float32,
            ) * HEAD_SIZE ** (-0.5)
            scores = jnp.where(allowed, scores, -jnp.inf)
            weights = jnp.exp(scores - jnp.max(scores, axis=1, keepdims=True))
            probs = (weights / jnp.sum(weights, axis=1, keepdims=True)).astype(jnp.bfloat16)
            context[half, :, columns] = jnp.dot(
                probs, pair_rows[:, HEAD_SIZE : 2 * HEAD_SIZE], preferred_element_type=jnp.float32
            ).astype(jnp.bfloat16)
            return carry

        lax.fori_loop(0, heads_width // HEAD_SIZE, one_head, 0)

    attend(1 - x)

    def pair_copy(k):
        return copy_to(
            pair_send.at[k], pair_receive.at[k], pair_sems.at[0, k], pair_sems.at[1, k], x_peer
        )

    def send_pair(k, carry):
        weight_chunk(k).wait()
        term = jnp.dot(context[1 - x], out_weight[k], preferred_element_type=jnp.float32)
        pair_send[k] = term.astype(jnp.bfloat16)
        pair_copy(k).start()
        return carry

    lax.fori_loop(0, chunks, send_pair, 0)
    attend(x)

    def line_copy(k, step):
        target = z_peer(step)
        source = line_send.at[k, pl.ds(pl.multiple_of(target * tokens, tokens), tokens)]
        return copy_to(
            source,
            line_receive.at[k, step - 1],
            line_send_sems.at[k, step - 1],
            line_receive_sems.at[k, step - 1],
            device(x, y, core, target),
        )

    def send_line(k, carry):
        term = jnp.dot(context[x], out_weight[k], preferred_element_type=jnp.float32)
        pair_copy(k).wait_recv()
        line_send[k] = (term + pair_receive[k].astype(jnp.float32)).astype(jnp.bfloat16)
        for step in (2, 1, 3):
            line_copy(k, step).start()
        return carry

    lax.fori_loop(0, chunks, send_line, 0)

    def finish(k, squares):
        columns = pl.ds(pl.multiple_of(k * chunk, chunk), chunk)
        total = line_send[k, pl.ds(pl.multiple_of(z * tokens, tokens), tokens)].astype(jnp.float32)
        for step in (1, 3, 2):
            line_copy(k, step).wait_recv()
            total = total + line_receive[k, step - 1].astype(jnp.float32)
        after = (residual_ref[:, columns].astype(jnp.float32) + total).astype(jnp.bfloat16)
        after_ref[:, columns] = after
        widened = after.astype(jnp.float32)
        return squares + jnp.sum(widened * widened, axis=1, keepdims=True)

    squares = lax.fori_loop(0, chunks, finish, jnp.zeros((tokens, 1), jnp.float32))
    inverse = lax.rsqrt(squares / model + 1e-06)
    scale = 448.0 / history_ref[grp]
    own_rows = pl.ds(pl.multiple_of(slot(x, y, core, z) * tokens, tokens), tokens)

    def normalize(k, highest):
        columns = pl.ds(pl.multiple_of(k * chunk, chunk), chunk)
        normed = after_ref[:, columns].astype(jnp.float32) * inverse * gain_ref[:, columns]
        rows[own_rows, columns] = jnp.clip(normed * scale, -448.0, 448.0).astype(jnp.bfloat16)
        return jnp.maximum(highest, jnp.max(jnp.abs(normed), axis=1, keepdims=True))

    highest = lax.fori_loop(0, chunks, normalize, jnp.zeros((tokens, 1), jnp.float32))

    rows[own_rows, pl.ds(model, 128)] = ranks_ref[...]

    started = []

    def pass_on(place, target, half=None, landing=0, allowed=None):
        number = len(started)

        def describe():
            source = block(place)
            if half is not None:
                source = source.at[pl.ds(half * (tokens // 2), tokens // 2)]
            return copy_to(
                source,
                source,
                row_send_sems.at[number],
                row_receive_sems.at[place, landing],
                target,
            )

        started.append((describe, allowed))
        if allowed is None:
            describe().start()
        else:
            pl.when(allowed)(lambda: describe().start())

    def arrived(place, half=None, landing=0):
        source = block(place)
        if half is not None:
            source = source.at[pl.ds(half * (tokens // 2), tokens // 2)]
        copy_to(
            source, source, row_send_sems.at[0], row_receive_sems.at[place, landing], sibling
        ).wait_recv()

    own = slot(x, y, core, z)
    pass_on(own, x_peer)
    pass_on(own, y_peer)
    pass_on(own, device(x, y, core, z + 1), allowed=z < 3)
    pass_on(own, device(x, y, core, z - 1), allowed=z > 0)
    pass_on(own, sibling)

    amaxes[sp] = jnp.broadcast_to(jnp.max(highest, axis=0, keepdims=True), amaxes.shape[1:])

    def amax_copy(step):
        target = lax.rem(sp + step, 8)
        return copy_to(
            amaxes.at[sp],
            amaxes.at[sp],
            amax_send_sems.at[step - 1],
            amax_receive_sems.at[step - 1],
            (grp, target),
        )

    for step in range(1, 8):
        amax_copy(step).start()

    for order in (1, 2, 3):
        place = slot(x, y, core, nearest[order])
        arrived(place)
        onward = 3 - z if order == 1 else 3 * (z - 1)
        pass_on(place, device(x, y, core, onward), allowed=z * (3 - z) > 0)
        pass_on(place, x_peer)
        pass_on(place, y_peer)
        pass_on(place, sibling)

    expert_copy.wait()
    expert = grp * 4 + z
    expert_lane = lax.broadcasted_iota(jnp.int32, (most, 128), 1) == expert
    expert_lane = expert_lane.astype(jnp.bfloat16)
    slots = lax.broadcasted_iota(jnp.int32, (most, tokens), 0)

    def compute(index, carry):
        other_core = lax.rem(core + index, 2)
        other_x = lax.rem(x + index // 2, 2)
        other_y = lax.rem(y + index // 4, 2)
        first = pl.multiple_of(slot(other_x, other_y, other_core, 0) * tokens, 4 * tokens)
        gate_up = jnp.dot(
            rows[pl.ds(first, 4 * tokens), pl.ds(0, model)],
            expert_weight[...],
            preferred_element_type=jnp.float32,
        )
        source = 2 * other_y + other_core
        unscale = history_ref[source] / 448.0
        gate = gate_up[:, :width] * unscale
        upward = gate_up[:, width:] * unscale
        hidden = (gate / (1.0 + jnp.exp(-gate)) * upward).astype(jnp.bfloat16)
        for line in range(4):
            origin = source * 8 + 2 * line + other_x
            ranks = lax.dot_general(
                expert_lane,
                rows[pl.ds(pl.multiple_of(first + line * tokens, tokens), tokens), pl.ds(model, 128)],
                (((1,), (1,)), ((), ())),
                preferred_element_type=jnp.float32,
            )
            picked = jnp.dot(
                (ranks.astype(jnp.int32) == slots).astype(jnp.bfloat16),
                hidden[line * tokens : (line + 1) * tokens],
                preferred_element_type=jnp.float32,
            )
            hidden_ref[pl.ds(pl.multiple_of(origin * most, most), most)] = picked.astype(
                jnp.bfloat16
            )
        return carry

    def sibling_group(x, y):
        for line in range(4):
            arrived(slot(x, y, 1 - core, line))

    lax.fori_loop(0, 1, compute, 0)
    sibling_group(x, y)
    lax.fori_loop(1, 2, compute, 0)

    for line in nearest:
        place = slot(1 - x, y, core, line)
        arrived(place)
        pass_on(place, y_peer, 0, 0)
        pass_on(place, sibling)
        place = slot(x, 1 - y, core, line)
        arrived(place)
        pass_on(place, x_peer, 1, 1)
        pass_on(place, sibling)
    sibling_group(1 - x, y)
    sibling_group(x, 1 - y)
    lax.fori_loop(2, 6, compute, 0)

    for line in nearest:
        place = slot(1 - x, 1 - y, core, line)
        arrived(place, 0, 0)
        arrived(place, 1, 1)
        pass_on(place, sibling)
    lax.fori_loop(6, 7, compute, 0)
    sibling_group(1 - x, 1 - y)
    lax.fori_loop(7, 8, compute, 0)

    for step in range(1, 8):
        amax_copy(step).wait_recv()
    amax_ref[...] = jnp.max(amaxes[...], axis=0)

    for step in range(1, 8):
        amax_copy(step).wait_send()
    for describe, allowed in started:
        if allowed is None:
            describe().wait_send()
        else:
            pl.when(allowed)(lambda describe=describe: describe().wait_send())
    for step in range(1, 8):
        for copy in head_copies(step, sp):
            copy.wait_send()

    def drain(k, carry):
        pair_copy(k).wait_send()
        for step in (1, 2, 3):
            line_copy(k, step).wait_send()
        return carry

    lax.fori_loop(0, chunks, drain, 0)


def whole_layer(
    queries,
    key_value_pairs,
    doc_ids,
    residual,
    norm_gain,
    amax_history,
    ranks,
    out_weight,
    expert_weight,
    devices,
    most,
):
    tokens, model = residual.shape
    block_width = out_weight.shape[0]
    width = expert_weight.shape[1] // 2
    chunks = 8
    chunk = model // chunks
    vmem = pl.BlockSpec(memory_space=pltpu.VMEM)
    smem = pl.BlockSpec(memory_space=pltpu.SMEM)
    hbm = pl.BlockSpec(memory_space=pl.ANY)
    dma = pltpu.SemaphoreType.DMA
    documents = jnp.broadcast_to(doc_ids.reshape(tokens, 1).astype(jnp.bfloat16), (tokens, 128))
    return pl.pallas_call(
        layer_kernel,
        out_shape=(
            jax.ShapeDtypeStruct((tokens, model), jnp.bfloat16),
            jax.ShapeDtypeStruct((devices * most, width), jnp.bfloat16),
            jax.ShapeDtypeStruct((8, 128), jnp.float32),
        ),
        in_specs=[hbm, vmem, vmem, vmem, vmem, smem, vmem, hbm, hbm],
        out_specs=(vmem, vmem, vmem),
        scratch_shapes=[
            pltpu.VMEM((8 * tokens, block_width), jnp.bfloat16),
            pltpu.VMEM((8 * tokens, 3 * HEAD_SIZE), jnp.bfloat16),
            pltpu.VMEM((KEY_VALUE_HEADS, tokens, 3 * HEAD_SIZE), jnp.bfloat16),
            pltpu.VMEM((2, 4 * tokens, block_width), jnp.bfloat16),
            pltpu.VMEM((chunks, block_width, chunk), jnp.bfloat16),
            pltpu.VMEM(expert_weight.shape, jnp.bfloat16),
            pltpu.VMEM((chunks, 4 * tokens, chunk), jnp.bfloat16),
            pltpu.VMEM((chunks, 4 * tokens, chunk), jnp.bfloat16),
            pltpu.VMEM((chunks, 4 * tokens, chunk), jnp.bfloat16),
            pltpu.VMEM((chunks, 3, tokens, chunk), jnp.bfloat16),
            pltpu.VMEM((devices * tokens, model + 128), jnp.bfloat16),
            pltpu.VMEM((8, 8, 128), jnp.float32),
            dma((chunks + 2,)),
            dma((2, chunks)),
            dma((chunks, 3)),
            dma((chunks, 3)),
            dma((40,)),
            dma((devices, 2)),
            dma((7,)),
            dma((7,)),
            dma((2, 7)),
            dma((2, 7)),
        ],
        compiler_params=pltpu.CompilerParams(
            collective_id=0, has_side_effects=True, vmem_limit_bytes=56 * 1024 * 1024
        ),
        cost_estimate=pl.CostEstimate(
            flops=2 * devices * tokens * model * 2 * width,
            bytes_accessed=12 * 1024 * 1024,
            transcendentals=devices * tokens * width,
        ),
        name="attend_project_norm_dispatch",
    )(
        queries,
        key_value_pairs,
        documents,
        residual,
        norm_gain.reshape(1, model),
        amax_history,
        ranks,
        out_weight,
        expert_weight,
    )


def rank_table(expert_ids, experts):
    local_row_count = expert_ids.shape[0]
    numbers = jnp.arange(128, dtype=jnp.int32)
    named = jnp.any(expert_ids[:, :, None] == numbers[None, None, :], axis=1)
    order = jnp.arange(local_row_count, dtype=jnp.int32)
    earlier = (order[None, :] < order[:, None]).astype(jnp.bfloat16)
    rank = jnp.dot(earlier, named.astype(jnp.bfloat16), preferred_element_type=jnp.float32)
    return jnp.where(named & (numbers < experts), rank, -1.0).astype(jnp.bfloat16)


def per_device(
    residual,
    queries,
    key_value_pairs,
    out_weight,
    norm_gain,
    amax_history,
    doc_ids,
    expert_ids,
    gate_up_weight,
):
    sequence_parallel_count = lax.axis_size("sp")
    grp_count = lax.axis_size("grp")
    local_row_count = residual.shape[0]
    heads_here = QUERY_HEAD_SLICE // sequence_parallel_count
    experts = grp_count * sequence_parallel_count // HALVES
    most_rows = max(2, local_row_count * TOP // experts)
    if (grp_count, sequence_parallel_count) == (4, 8):
        after_attention, expert_hidden, highest = whole_layer(
            queries,
            key_value_pairs,
            doc_ids,
            residual,
            norm_gain,
            amax_history,
            rank_table(expert_ids, experts),
            out_weight,
            gate_up_weight[0],
            grp_count * sequence_parallel_count,
            most_rows,
        )
        return after_attention, expert_hidden[None], highest[0, :1]
    query_local = queries.reshape(local_row_count, sequence_parallel_count, heads_here * HEAD_SIZE)
    pair_replicas = jnp.repeat(
        key_value_pairs.reshape(local_row_count, KEY_VALUE_HEADS, 2 * HEAD_SIZE),
        sequence_parallel_count // KEY_VALUE_HEADS,
        axis=1,
    )
    doc_copies = jnp.broadcast_to(
        doc_ids.reshape(local_row_count, 1, 1), (local_row_count, sequence_parallel_count, 1)
    )
    query_heads, pair_head, doc_column = (
        lax.all_to_all(query_local, "sp", split_axis=1, concat_axis=0, tiled=True),
        lax.all_to_all(pair_replicas, "sp", split_axis=1, concat_axis=0, tiled=True),
        lax.all_to_all(doc_copies, "sp", split_axis=1, concat_axis=0, tiled=True),
    )
    slice_length = query_heads.shape[0]
    pair_head = pair_head.reshape(slice_length, 2 * HEAD_SIZE)
    documents = doc_column.reshape(slice_length)
    query_heads = query_heads.reshape(slice_length, heads_here, HEAD_SIZE)
    key_rows = pair_head[:, :HEAD_SIZE]
    value_rows = pair_head[:, HEAD_SIZE:]
    block_rows = min(512, slice_length)
    positions = jnp.arange(slice_length, dtype=jnp.int32)

    def attend(block_index):
        offset = block_index * block_rows
        query_block = lax.dynamic_slice_in_dim(query_heads, offset, block_rows, 0)
        row_positions = offset + jnp.arange(block_rows, dtype=jnp.int32)
        row_documents = lax.dynamic_slice_in_dim(documents, offset, block_rows, 0)
        allowed = (positions[None, :] <= row_positions[:, None]) & (
            documents[None, :] == row_documents[:, None]
        )
        scores = jnp.einsum(
            "bhd,kd->hbk", query_block, key_rows, preferred_element_type=jnp.float32
        ) * HEAD_SIZE ** (-0.5)
        scores = jnp.where(allowed[None], scores, -jnp.inf)
        highest = jnp.max(scores, axis=2, keepdims=True)
        weights = jnp.exp(scores - highest)
        probs = (weights / jnp.sum(weights, axis=2, keepdims=True)).astype(jnp.bfloat16)
        return jnp.einsum(
            "hbk,kd->bhd", probs, value_rows, preferred_element_type=jnp.float32
        ).astype(jnp.bfloat16)

    context = lax.map(attend, jnp.arange(slice_length // block_rows, dtype=jnp.int32))
    block_width = heads_here * HEAD_SIZE
    context = context.reshape(slice_length, block_width)
    projected = lax.psum_scatter(
        jnp.dot(context, out_weight, preferred_element_type=jnp.float32).astype(jnp.bfloat16),
        "sp",
        scatter_dimension=0,
        tiled=True,
    ).astype(jnp.float32)
    after_attention = (residual.astype(jnp.float32) + projected).astype(jnp.bfloat16)
    widened = after_attention.astype(jnp.float32)
    normed = (
        widened * lax.rsqrt(jnp.mean(widened * widened, axis=1, keepdims=True) + 1e-06) * norm_gain
    )
    group_amax = lax.pmax(jnp.max(jnp.abs(normed)).reshape(1), "sp")
    own_history = lax.dynamic_index_in_dim(amax_history, lax.axis_index("grp"), 0, False)
    quantized = jnp.clip(normed * (448.0 / own_history), -448.0, 448.0).astype(jnp.bfloat16)
    routing = expert_ids.reshape(local_row_count * TOP)
    one_hot = (routing[:, None] == jnp.arange(experts, dtype=jnp.int32)[None, :]).astype(jnp.int32)
    rank = jnp.sum((jnp.cumsum(one_hot, axis=0) - one_hot) * one_hot, axis=1)
    slot_index = routing * most_rows + rank
    picker = jnp.arange(experts * most_rows, dtype=jnp.int32)[:, None] == slot_index[None, :]
    picker = jnp.sum(
        picker.reshape(experts * most_rows, local_row_count, TOP).astype(jnp.int32), axis=2
    ).astype(jnp.bfloat16)
    outgoing = jnp.dot(picker, quantized, preferred_element_type=jnp.float32).astype(jnp.bfloat16)
    outgoing = outgoing.reshape(grp_count, experts // grp_count, most_rows, outgoing.shape[1])
    arrived = lax.all_to_all(outgoing, "grp", split_axis=0, concat_axis=0, tiled=True)
    width_model = arrived.shape[3]
    copies = jnp.repeat(arrived, HALVES, axis=1)
    slot_rows = lax.all_to_all(copies, "sp", split_axis=1, concat_axis=1, tiled=True)
    total_rows = grp_count * sequence_parallel_count * most_rows
    flat_rows = slot_rows.reshape(total_rows, width_model)
    unscale = jnp.repeat(amax_history / 448.0, sequence_parallel_count * most_rows)[:, None]
    weight = gate_up_weight[0]
    expert_hidden = activate(flat_rows, unscale, weight)
    return (
        after_attention,
        expert_hidden.reshape(1, total_rows, expert_hidden.shape[1]),
        group_amax,
    )


def solution(mesh):
    in_specs = (
        P(("grp", "sp"), None),
        P(("grp", "sp"), None),
        P(("grp", "sp"), None),
        P("sp", None),
        P(),
        P(),
        P("grp", "sp"),
        P(("grp", "sp"), None),
        P(("grp", "sp"), None, None),
    )
    out_specs = (P(("grp", "sp"), None), P(("grp", "sp"), None, None), P("grp"))
    return jax.shard_map(
        per_device, mesh=mesh, in_specs=in_specs, out_specs=out_specs, check_vma=False
    )
```

```python
import jax
import jax.numpy as jnp
from jax import lax
from jax.experimental import pallas as pl
from jax.experimental.pallas import tpu as pltpu
from jax.sharding import PartitionSpec as P

QUERY_HEAD_SLICE = 32
KEY_VALUE_HEADS = 4
HEAD_SIZE = 128
TOP = 8
HALVES = 2


def activate(rows, unscale, weight):
    width = weight.shape[1] // 2
    gate_up = jnp.dot(rows, weight, preferred_element_type=jnp.float32)
    gate = gate_up[:, :width] * unscale
    upward = gate_up[:, width:] * unscale
    return (jax.nn.silu(gate) * upward).astype(jnp.bfloat16)


def copy_to(source, target, send, receive, device):
    return pltpu.make_async_remote_copy(
        src_ref=source,
        dst_ref=target,
        send_sem=send,
        recv_sem=receive,
        device_id=device,
        device_id_type=pl.DeviceIdType.MESH,
    )


def layer_kernel(
    queries_ref,
    pairs_ref,
    documents_ref,
    residual_ref,
    gain_ref,
    history_ref,
    expert_ids_ref,
    out_weight_ref,
    expert_weight_ref,
    after_ref,
    hidden_ref,
    amax_ref,
    query_rows,
    pair_rows,
    pair_blocks,
    document_tiles,
    context,
    out_weight,
    expert_weight,
    pair_send,
    pair_receive,
    line_send,
    line_receive,
    rows,
    amaxes,
    local_sem,
    pair_sems,
    line_send_sems,
    line_receive_sems,
    row_send_sems,
    row_receive_sems,
    amax_send_sems,
    amax_receive_sems,
    head_send_sems,
    head_receive_sems,
):
    grp, sp = lax.axis_index("grp"), lax.axis_index("sp")
    y, core = grp // 2, grp % 2
    z, x = sp // 2, sp % 2
    tokens, model = residual_ref.shape
    chunks, _, chunk = pair_send.shape
    width = hidden_ref.shape[1]
    most = hidden_ref.shape[0] * tokens // rows.shape[0]
    heads_width = query_rows.shape[1]
    nearest = (z, z + 1 - 2 * (z % 2), 2 - z // 2, 3 * (1 - z // 2))

    def device(x, y, core, z):
        return (2 * y + core, 2 * z + x)

    def slot(x, y, core, z):
        return ((y * 2 + x) * 2 + core) * 4 + z

    def block(place):
        return rows.at[pl.ds(pl.multiple_of(place * tokens, tokens), tokens)]

    def z_peer(step):
        return lax.rem(z + step, 4)

    sibling = device(x, y, 1 - core, z)
    x_peer = device(1 - x, y, core, z)
    y_peer = device(x, 1 - y, core, z)

    def weight_chunk(k):
        columns = pl.ds(pl.multiple_of(k * chunk, chunk), chunk)
        return pltpu.make_async_copy(
            out_weight_ref.at[:, columns], out_weight.at[k], local_sem.at[k]
        )

    expert_copy = pltpu.make_async_copy(expert_weight_ref, expert_weight, local_sem.at[chunks])
    for k in range(chunks):
        weight_chunk(k).start()
    expert_copy.start()

    diagonal = lax.broadcasted_iota(jnp.int32, (tokens, 128), 1) == lax.broadcasted_iota(
        jnp.int32, (tokens, 128), 0
    )
    own_documents = jnp.broadcast_to(documents_ref[...].astype(jnp.float32), (16, tokens))
    document_tiles[sp] = jnp.dot(
        own_documents.astype(jnp.bfloat16),
        diagonal.astype(jnp.bfloat16),
        preferred_element_type=jnp.float32,
    ).astype(jnp.bfloat16)
    for head in range(KEY_VALUE_HEADS):
        pair_blocks[head] = pairs_ref[:, head * 2 * HEAD_SIZE : (head + 1) * 2 * HEAD_SIZE]

    barrier = pltpu.get_barrier_semaphore()
    partners = [sibling, x_peer, y_peer]
    for step in (1, 2, 3):
        partners.append(device(x, y, core, z_peer(step)))
        partners.append(device(1 - x, y, core, z_peer(step)))
    for partner in partners:
        pl.semaphore_signal(
            barrier, inc=1, device_id=partner, device_id_type=pl.DeviceIdType.MESH
        )
    pl.semaphore_wait(barrier, len(partners))

    def token_rows(member):
        place = (member % 2) * 4 + member // 2
        return pl.ds(pl.multiple_of(place * tokens, tokens), tokens)

    def query_columns(member):
        return queries_ref.at[
            :, pl.ds(pl.multiple_of(member * heads_width, heads_width), heads_width)
        ]

    def query_copy(step, origin):
        target = lax.rem(sp + step, 8)
        return copy_to(
            query_columns(target),
            query_rows.at[token_rows(origin)],
            head_send_sems.at[1, step - 1],
            head_receive_sems.at[1, step - 1],
            (grp, target),
        )

    def document_copy(step, origin):
        return copy_to(
            document_tiles.at[sp],
            document_tiles.at[origin],
            head_send_sems.at[2, step - 1],
            head_receive_sems.at[2, step - 1],
            (grp, lax.rem(sp + step, 8)),
        )

    def pair_line_copy(step, origin):
        target = z_peer(step)
        return copy_to(
            pair_blocks.at[target],
            pair_rows.at[token_rows(origin)],
            head_send_sems.at[0, step - 1],
            head_receive_sems.at[0, step - 1],
            device(x, y, core, target),
        )

    def pair_across_copy(step, origin_x):
        there = token_rows(2 * z_peer(4 - step) + origin_x)
        return copy_to(
            pair_rows.at[there],
            pair_rows.at[there],
            head_send_sems.at[0, 3 + step],
            head_receive_sems.at[0, 3 + step],
            x_peer,
        )

    for step in range(1, 8):
        document_copy(step, sp).start()
    for step in (2, 1, 3):
        pair_line_copy(step, sp).start()
    for step in (4, 3, 5, 2, 6, 1, 7):
        query_copy(step, sp).start()
    own_queries = pltpu.make_async_copy(
        query_columns(sp), query_rows.at[token_rows(sp)], local_sem.at[chunks + 1]
    )
    own_queries.start()
    pair_rows[token_rows(sp)] = pair_blocks[z]
    pair_across_copy(0, x).start()
    for step in (1, 3, 2):
        pair_line_copy(step, 2 * z_peer(4 - step) + x).wait_recv()
        pair_across_copy(step, x).start()
    own_queries.wait()
    for step in range(1, 8):
        document_copy(step, lax.rem(sp + 8 - step, 8)).wait_recv()
    for step in range(4):
        pair_across_copy(step, 1 - x).wait_recv()
    for step in range(1, 8):
        query_copy(step, lax.rem(sp + 8 - step, 8)).wait_recv()

    column_documents = jnp.zeros((16, 8 * tokens), jnp.float32)
    for member in range(8):
        place = (member % 2) * 4 + member // 2
        shifted = lax.broadcasted_iota(jnp.int32, (128, 8 * tokens), 1) == (
            lax.broadcasted_iota(jnp.int32, (128, 8 * tokens), 0) + place * tokens
        )
        inside = lax.broadcasted_iota(jnp.int32, (128, 8 * tokens), 0) < tokens
        column_documents = column_documents + jnp.dot(
            document_tiles[member],
            (shifted & inside).astype(jnp.bfloat16),
            preferred_element_type=jnp.float32,
        )
    column_documents = column_documents[:1]

    def attend(half):
        count = 4 * tokens
        here = pl.ds(pl.multiple_of(half * count, count), count)
        row = lax.broadcasted_iota(jnp.int32, (count, 1), 0)
        column = lax.broadcasted_iota(jnp.int32, (1, 2 * count), 1)
        row_position = (lax.div(row, tokens) * 2 + half) * tokens + lax.rem(row, tokens)
        column_half = lax.div(column, count)
        column_place = lax.rem(column, count)
        column_position = (lax.div(column_place, tokens) * 2 + column_half) * tokens + lax.rem(
            column_place, tokens
        )
        same_token = column == row + half * count
        row_documents = jnp.sum(
            jnp.where(same_token, column_documents, 0.0), axis=1, keepdims=True
        )
        allowed = (column_position <= row_position) & (row_documents == column_documents)

        def one_head(head, carry):
            columns = pl.ds(pl.multiple_of(head * HEAD_SIZE, HEAD_SIZE), HEAD_SIZE)
            scores = lax.dot_general(
                query_rows[here, columns],
                pair_rows[:, :HEAD_SIZE],
                (((1,), (1,)), ((), ())),
                preferred_element_type=jnp.float32,
            ) * HEAD_SIZE ** (-0.5)
            scores = jnp.where(allowed, scores, -jnp.inf)
            weights = jnp.exp(scores - jnp.max(scores, axis=1, keepdims=True))
            probs = (weights / jnp.sum(weights, axis=1, keepdims=True)).astype(jnp.bfloat16)
            context[half, :, columns] = jnp.dot(
                probs, pair_rows[:, HEAD_SIZE : 2 * HEAD_SIZE], preferred_element_type=jnp.float32
            ).astype(jnp.bfloat16)
            return carry

        lax.fori_loop(0, heads_width // HEAD_SIZE, one_head, 0)

    attend(1 - x)

    def pair_copy(k):
        return copy_to(
            pair_send.at[k], pair_receive.at[k], pair_sems.at[0, k], pair_sems.at[1, k], x_peer
        )

    def send_pair(k, carry):
        weight_chunk(k).wait()
        term = jnp.dot(context[1 - x], out_weight[k], preferred_element_type=jnp.float32)
        pair_send[k] = term.astype(jnp.bfloat16)
        pair_copy(k).start()
        return carry

    lax.fori_loop(0, chunks, send_pair, 0)
    attend(x)

    def line_copy(k, step):
        target = z_peer(step)
        source = line_send.at[k, pl.ds(pl.multiple_of(target * tokens, tokens), tokens)]
        return copy_to(
            source,
            line_receive.at[k, step - 1],
            line_send_sems.at[k, step - 1],
            line_receive_sems.at[k, step - 1],
            device(x, y, core, target),
        )

    def send_line(k, carry):
        term = jnp.dot(context[x], out_weight[k], preferred_element_type=jnp.float32)
        pair_copy(k).wait_recv()
        line_send[k] = (term + pair_receive[k].astype(jnp.float32)).astype(jnp.bfloat16)
        for step in (2, 1, 3):
            line_copy(k, step).start()
        return carry

    lax.fori_loop(0, chunks, send_line, 0)

    def finish(k, squares):
        columns = pl.ds(pl.multiple_of(k * chunk, chunk), chunk)
        total = line_send[k, pl.ds(pl.multiple_of(z * tokens, tokens), tokens)].astype(jnp.float32)
        for step in (1, 3, 2):
            line_copy(k, step).wait_recv()
            total = total + line_receive[k, step - 1].astype(jnp.float32)
        after = (residual_ref[:, columns].astype(jnp.float32) + total).astype(jnp.bfloat16)
        after_ref[:, columns] = after
        widened = after.astype(jnp.float32)
        return squares + jnp.sum(widened * widened, axis=1, keepdims=True)

    squares = lax.fori_loop(0, chunks, finish, jnp.zeros((tokens, 1), jnp.float32))
    inverse = lax.rsqrt(squares / model + 1e-06)
    scale = 448.0 / history_ref[grp]
    own_rows = pl.ds(pl.multiple_of(slot(x, y, core, z) * tokens, tokens), tokens)

    def normalize(k, highest):
        columns = pl.ds(pl.multiple_of(k * chunk, chunk), chunk)
        normed = after_ref[:, columns].astype(jnp.float32) * inverse * gain_ref[:, columns]
        rows[own_rows, columns] = jnp.clip(normed * scale, -448.0, 448.0).astype(jnp.bfloat16)
        return jnp.maximum(highest, jnp.max(jnp.abs(normed), axis=1, keepdims=True))

    highest = lax.fori_loop(0, chunks, normalize, jnp.zeros((tokens, 1), jnp.float32))

    earlier = lax.broadcasted_iota(jnp.int32, (tokens, tokens), 1) < lax.broadcasted_iota(
        jnp.int32, (tokens, tokens), 0
    )
    numbers = lax.broadcasted_iota(jnp.int32, (tokens, 128), 1)
    named = jnp.zeros((tokens, 128), jnp.float32)
    for choice in range(expert_ids_ref.shape[1]):
        chosen = expert_ids_ref[:, choice : choice + 1] == numbers
        named = jnp.maximum(named, jnp.where(chosen, 1.0, 0.0))
    rank = jnp.dot(
        earlier.astype(jnp.bfloat16), named.astype(jnp.bfloat16), preferred_element_type=jnp.float32
    )
    rows[own_rows, pl.ds(model, 128)] = jnp.where(named > 0.5, rank, -1.0).astype(jnp.bfloat16)

    started = []

    def pass_on(place, target, half=None, landing=0, allowed=None):
        number = len(started)

        def describe():
            source = block(place)
            if half is not None:
                source = source.at[pl.ds(half * (tokens // 2), tokens // 2)]
            return copy_to(
                source,
                source,
                row_send_sems.at[number],
                row_receive_sems.at[place, landing],
                target,
            )

        started.append((describe, allowed))
        if allowed is None:
            describe().start()
        else:
            pl.when(allowed)(lambda: describe().start())

    def arrived(place, half=None, landing=0):
        source = block(place)
        if half is not None:
            source = source.at[pl.ds(half * (tokens // 2), tokens // 2)]
        copy_to(
            source, source, row_send_sems.at[0], row_receive_sems.at[place, landing], sibling
        ).wait_recv()

    own = slot(x, y, core, z)
    pass_on(own, x_peer)
    pass_on(own, y_peer)
    pass_on(own, device(x, y, core, z + 1), allowed=z < 3)
    pass_on(own, device(x, y, core, z - 1), allowed=z > 0)
    pass_on(own, sibling)

    amaxes[sp] = jnp.broadcast_to(jnp.max(highest, axis=0, keepdims=True), amaxes.shape[1:])

    def amax_copy(step):
        target = lax.rem(sp + step, 8)
        return copy_to(
            amaxes.at[sp],
            amaxes.at[sp],
            amax_send_sems.at[step - 1],
            amax_receive_sems.at[step - 1],
            (grp, target),
        )

    for step in range(1, 8):
        amax_copy(step).start()

    for order in (1, 2, 3):
        place = slot(x, y, core, nearest[order])
        arrived(place)
        onward = 3 - z if order == 1 else 3 * (z - 1)
        pass_on(place, device(x, y, core, onward), allowed=z * (3 - z) > 0)
        pass_on(place, x_peer)
        pass_on(place, y_peer)
        pass_on(place, sibling)

    expert_copy.wait()
    expert = grp * 4 + z
    expert_lane = lax.broadcasted_iota(jnp.int32, (most, 128), 1) == expert
    expert_lane = expert_lane.astype(jnp.bfloat16)
    slots = lax.broadcasted_iota(jnp.int32, (most, tokens), 0)

    def compute(index, carry):
        other_core = lax.rem(core + index, 2)
        other_x = lax.rem(x + index // 2, 2)
        other_y = lax.rem(y + index // 4, 2)
        first = pl.multiple_of(slot(other_x, other_y, other_core, 0) * tokens, 4 * tokens)
        gate_up = jnp.dot(
            rows[pl.ds(first, 4 * tokens), pl.ds(0, model)],
            expert_weight[...],
            preferred_element_type=jnp.float32,
        )
        source = 2 * other_y + other_core
        unscale = history_ref[source] / 448.0
        gate = gate_up[:, :width] * unscale
        upward = gate_up[:, width:] * unscale
        hidden = (gate / (1.0 + jnp.exp(-gate)) * upward).astype(jnp.bfloat16)
        for line in range(4):
            origin = source * 8 + 2 * line + other_x
            ranks = lax.dot_general(
                expert_lane,
                rows[pl.ds(pl.multiple_of(first + line * tokens, tokens), tokens), pl.ds(model, 128)],
                (((1,), (1,)), ((), ())),
                preferred_element_type=jnp.float32,
            )
            picked = jnp.dot(
                (ranks.astype(jnp.int32) == slots).astype(jnp.bfloat16),
                hidden[line * tokens : (line + 1) * tokens],
                preferred_element_type=jnp.float32,
            )
            hidden_ref[pl.ds(pl.multiple_of(origin * most, most), most)] = picked.astype(
                jnp.bfloat16
            )
        return carry

    def sibling_group(x, y):
        for line in range(4):
            arrived(slot(x, y, 1 - core, line))

    for number, line in enumerate(nearest):
        if number == 3:
            sibling_group(x, y)
            lax.fori_loop(0, 2, compute, 0)
        place = slot(1 - x, y, core, line)
        arrived(place)
        pass_on(place, y_peer, 0, 0)
        pass_on(place, sibling)
        place = slot(x, 1 - y, core, line)
        arrived(place)
        pass_on(place, x_peer, 1, 1)
        pass_on(place, sibling)
    sibling_group(1 - x, y)
    sibling_group(x, 1 - y)
    lax.fori_loop(2, 6, compute, 0)

    for line in nearest:
        place = slot(1 - x, 1 - y, core, line)
        arrived(place, 0, 0)
        arrived(place, 1, 1)
        pass_on(place, sibling)
    lax.fori_loop(6, 7, compute, 0)
    sibling_group(1 - x, 1 - y)
    lax.fori_loop(7, 8, compute, 0)

    for step in range(1, 8):
        amax_copy(step).wait_recv()
    amax_ref[...] = jnp.max(amaxes[...], axis=0)

    for step in range(1, 8):
        amax_copy(step).wait_send()
    for describe, allowed in started:
        if allowed is None:
            describe().wait_send()
        else:
            pl.when(allowed)(lambda describe=describe: describe().wait_send())
    for step in range(1, 8):
        query_copy(step, sp).wait_send()
        document_copy(step, sp).wait_send()
    for step in range(1, 4):
        pair_line_copy(step, sp).wait_send()
    for step in range(4):
        pair_across_copy(step, x).wait_send()

    def drain(k, carry):
        pair_copy(k).wait_send()
        for step in (1, 2, 3):
            line_copy(k, step).wait_send()
        return carry

    lax.fori_loop(0, chunks, drain, 0)


def whole_layer(
    queries,
    key_value_pairs,
    doc_ids,
    residual,
    norm_gain,
    amax_history,
    expert_ids,
    out_weight,
    expert_weight,
    devices,
    most,
):
    tokens, model = residual.shape
    block_width = out_weight.shape[0]
    width = expert_weight.shape[1] // 2
    chunks = 8
    chunk = model // chunks
    vmem = pl.BlockSpec(memory_space=pltpu.VMEM)
    smem = pl.BlockSpec(memory_space=pltpu.SMEM)
    hbm = pl.BlockSpec(memory_space=pl.ANY)
    dma = pltpu.SemaphoreType.DMA
    return pl.pallas_call(
        layer_kernel,
        out_shape=(
            jax.ShapeDtypeStruct((tokens, model), jnp.bfloat16),
            jax.ShapeDtypeStruct((devices * most, width), jnp.bfloat16),
            jax.ShapeDtypeStruct((8, 128), jnp.float32),
        ),
        in_specs=[hbm, vmem, vmem, vmem, vmem, smem, vmem, hbm, hbm],
        out_specs=(vmem, vmem, vmem),
        scratch_shapes=[
            pltpu.VMEM((8 * tokens, block_width), jnp.bfloat16),
            pltpu.VMEM((8 * tokens, 2 * HEAD_SIZE), jnp.bfloat16),
            pltpu.VMEM((KEY_VALUE_HEADS, tokens, 2 * HEAD_SIZE), jnp.bfloat16),
            pltpu.VMEM((8, 16, 128), jnp.bfloat16),
            pltpu.VMEM((2, 4 * tokens, block_width), jnp.bfloat16),
            pltpu.VMEM((chunks, block_width, chunk), jnp.bfloat16),
            pltpu.VMEM(expert_weight.shape, jnp.bfloat16),
            pltpu.VMEM((chunks, 4 * tokens, chunk), jnp.bfloat16),
            pltpu.VMEM((chunks, 4 * tokens, chunk), jnp.bfloat16),
            pltpu.VMEM((chunks, 4 * tokens, chunk), jnp.bfloat16),
            pltpu.VMEM((chunks, 3, tokens, chunk), jnp.bfloat16),
            pltpu.VMEM((devices * tokens, model + 128), jnp.bfloat16),
            pltpu.VMEM((8, 8, 128), jnp.float32),
            dma((chunks + 2,)),
            dma((2, chunks)),
            dma((chunks, 3)),
            dma((chunks, 3)),
            dma((80,)),
            dma((devices, 3)),
            dma((7,)),
            dma((7,)),
            dma((3, 7)),
            dma((3, 7)),
        ],
        compiler_params=pltpu.CompilerParams(
            collective_id=0, has_side_effects=True, vmem_limit_bytes=56 * 1024 * 1024
        ),
        cost_estimate=pl.CostEstimate(
            flops=2 * devices * tokens * model * 2 * width,
            bytes_accessed=12 * 1024 * 1024,
            transcendentals=devices * tokens * width,
        ),
        name="attend_project_norm_dispatch",
    )(
        queries,
        key_value_pairs,
        doc_ids,
        residual,
        norm_gain.reshape(1, model),
        amax_history,
        expert_ids,
        out_weight,
        expert_weight,
    )


def per_device(
    residual,
    queries,
    key_value_pairs,
    out_weight,
    norm_gain,
    amax_history,
    doc_ids,
    expert_ids,
    gate_up_weight,
):
    sequence_parallel_count = lax.axis_size("sp")
    grp_count = lax.axis_size("grp")
    local_row_count = residual.shape[0]
    heads_here = QUERY_HEAD_SLICE // sequence_parallel_count
    experts = grp_count * sequence_parallel_count // HALVES
    most_rows = max(2, local_row_count * TOP // experts)
    if (grp_count, sequence_parallel_count) == (4, 8):
        after_attention, expert_hidden, highest = whole_layer(
            queries,
            key_value_pairs,
            doc_ids,
            residual,
            norm_gain,
            amax_history,
            expert_ids,
            out_weight,
            gate_up_weight[0],
            grp_count * sequence_parallel_count,
            most_rows,
        )
        return after_attention, expert_hidden[None], highest[0, :1]
    query_local = queries.reshape(local_row_count, sequence_parallel_count, heads_here * HEAD_SIZE)
    pair_replicas = jnp.repeat(
        key_value_pairs.reshape(local_row_count, KEY_VALUE_HEADS, 2 * HEAD_SIZE),
        sequence_parallel_count // KEY_VALUE_HEADS,
        axis=1,
    )
    doc_copies = jnp.broadcast_to(
        doc_ids.reshape(local_row_count, 1, 1), (local_row_count, sequence_parallel_count, 1)
    )
    query_heads, pair_head, doc_column = (
        lax.all_to_all(query_local, "sp", split_axis=1, concat_axis=0, tiled=True),
        lax.all_to_all(pair_replicas, "sp", split_axis=1, concat_axis=0, tiled=True),
        lax.all_to_all(doc_copies, "sp", split_axis=1, concat_axis=0, tiled=True),
    )
    slice_length = query_heads.shape[0]
    pair_head = pair_head.reshape(slice_length, 2 * HEAD_SIZE)
    documents = doc_column.reshape(slice_length)
    query_heads = query_heads.reshape(slice_length, heads_here, HEAD_SIZE)
    key_rows = pair_head[:, :HEAD_SIZE]
    value_rows = pair_head[:, HEAD_SIZE:]
    block_rows = min(512, slice_length)
    positions = jnp.arange(slice_length, dtype=jnp.int32)

    def attend(block_index):
        offset = block_index * block_rows
        query_block = lax.dynamic_slice_in_dim(query_heads, offset, block_rows, 0)
        row_positions = offset + jnp.arange(block_rows, dtype=jnp.int32)
        row_documents = lax.dynamic_slice_in_dim(documents, offset, block_rows, 0)
        allowed = (positions[None, :] <= row_positions[:, None]) & (
            documents[None, :] == row_documents[:, None]
        )
        scores = jnp.einsum(
            "bhd,kd->hbk", query_block, key_rows, preferred_element_type=jnp.float32
        ) * HEAD_SIZE ** (-0.5)
        scores = jnp.where(allowed[None], scores, -jnp.inf)
        highest = jnp.max(scores, axis=2, keepdims=True)
        weights = jnp.exp(scores - highest)
        probs = (weights / jnp.sum(weights, axis=2, keepdims=True)).astype(jnp.bfloat16)
        return jnp.einsum(
            "hbk,kd->bhd", probs, value_rows, preferred_element_type=jnp.float32
        ).astype(jnp.bfloat16)

    context = lax.map(attend, jnp.arange(slice_length // block_rows, dtype=jnp.int32))
    block_width = heads_here * HEAD_SIZE
    context = context.reshape(slice_length, block_width)
    projected = lax.psum_scatter(
        jnp.dot(context, out_weight, preferred_element_type=jnp.float32).astype(jnp.bfloat16),
        "sp",
        scatter_dimension=0,
        tiled=True,
    ).astype(jnp.float32)
    after_attention = (residual.astype(jnp.float32) + projected).astype(jnp.bfloat16)
    widened = after_attention.astype(jnp.float32)
    normed = (
        widened * lax.rsqrt(jnp.mean(widened * widened, axis=1, keepdims=True) + 1e-06) * norm_gain
    )
    group_amax = lax.pmax(jnp.max(jnp.abs(normed)).reshape(1), "sp")
    own_history = lax.dynamic_index_in_dim(amax_history, lax.axis_index("grp"), 0, False)
    quantized = jnp.clip(normed * (448.0 / own_history), -448.0, 448.0).astype(jnp.bfloat16)
    routing = expert_ids.reshape(local_row_count * TOP)
    one_hot = (routing[:, None] == jnp.arange(experts, dtype=jnp.int32)[None, :]).astype(jnp.int32)
    rank = jnp.sum((jnp.cumsum(one_hot, axis=0) - one_hot) * one_hot, axis=1)
    slot_index = routing * most_rows + rank
    picker = jnp.arange(experts * most_rows, dtype=jnp.int32)[:, None] == slot_index[None, :]
    picker = jnp.sum(
        picker.reshape(experts * most_rows, local_row_count, TOP).astype(jnp.int32), axis=2
    ).astype(jnp.bfloat16)
    outgoing = jnp.dot(picker, quantized, preferred_element_type=jnp.float32).astype(jnp.bfloat16)
    outgoing = outgoing.reshape(grp_count, experts // grp_count, most_rows, outgoing.shape[1])
    arrived = lax.all_to_all(outgoing, "grp", split_axis=0, concat_axis=0, tiled=True)
    width_model = arrived.shape[3]
    copies = jnp.repeat(arrived, HALVES, axis=1)
    slot_rows = lax.all_to_all(copies, "sp", split_axis=1, concat_axis=1, tiled=True)
    total_rows = grp_count * sequence_parallel_count * most_rows
    flat_rows = slot_rows.reshape(total_rows, width_model)
    unscale = jnp.repeat(amax_history / 448.0, sequence_parallel_count * most_rows)[:, None]
    weight = gate_up_weight[0]
    expert_hidden = activate(flat_rows, unscale, weight)
    return (
        after_attention,
        expert_hidden.reshape(1, total_rows, expert_hidden.shape[1]),
        group_amax,
    )


def solution(mesh):
    in_specs = (
        P(("grp", "sp"), None),
        P(("grp", "sp"), None),
        P(("grp", "sp"), None),
        P("sp", None),
        P(),
        P(),
        P("grp", "sp"),
        P(("grp", "sp"), None),
        P(("grp", "sp"), None, None),
    )
    out_specs = (P(("grp", "sp"), None), P(("grp", "sp"), None, None), P("grp"))
    return jax.shard_map(
        per_device, mesh=mesh, in_specs=in_specs, out_specs=out_specs, check_vma=False
    )
```
